256 devices in a mesh: dp: 16 (over z, y_lo), tensor: 16 (over y_hi, x, core).
Axes of the slice: x: 4, y: 4 (y_hi: 2, y_lo: 2; y = y_hi * 2 + y_lo), z: 8, core: 2. Of those that a mesh axis runs over, the one named last changes fastest.
Arguments:
- tokens: bfloat16 [16, 1024, 8192], P('dp', 'tensor'), may hold values from -6 to 6
- cotangent: bfloat16 [16, 1024, 14336], P('dp', 'tensor'), may hold values from -6 to 6
- weights: bfloat16 [16, 112, 2, 2, 128, 128], P('dp', 'tensor'), may hold values from -6 to 6
- momentum: bfloat16 [16, 112, 2, 2, 128, 128], P('dp', 'tensor'), may hold values from -4 to 4
- pattern: int32 [112, 2], P('tensor'), may hold values from 0 to 63, all different within a row
- step: int32 [], replicated, may hold values from 0 to 4095
Outputs:
- hidden: bfloat16 [16, 1024, 14336], P('dp', 'tensor')
- new_weights: bfloat16 [16, 112, 2, 2, 128, 128], P('dp', 'tensor')
- new_momentum: bfloat16 [16, 112, 2, 2, 128, 128], P('dp', 'tensor')
The draws below stay inside these ranges and needn't reach their ends.
Inputs may be any that keep to these rules, and one draw needn't show every extreme that they name: `pattern`: each row names 2 different input blocks; every input block is named by some row.
All inputs are finite; a program needn't handle non-finite values.
Results may differ from the reference program's by a relative error of at most 0.0058.
Values may be sent and summed in bfloat16 or wider, within the bound.
No kernel may reach another device: no remote copies, remote signals or barrier semaphores. Data moves between devices by JAX's collectives and lax.ppermute only.
A program may use at most 128 MiB of HBM per device.

```python
from functools import partial
import jax
import jax.numpy as jnp
from jax import lax

D = 8192
FF = 14336
BLOCK = 128
KB = 2
TOKENS = 1024
DB = 64
FFB = 112
N_DP = 16


def block_scale(stream_key, dims, split, low, high):
    def one(axis_at, parts):
        draws = jax.random.uniform(jax.random.fold_in(jax.random.fold_in(stream_key, 6), axis_at), (parts,), jnp.float32, low / len(split), high / len(split))
        return jnp.repeat(jnp.exp(draws), dims[axis_at] // parts).reshape((-1,) + (1,) * (len(dims) - axis_at - 1))

    loudness = one(*split[0])
    for cut in split[1:]:
        loudness = loudness * one(*cut)
    return loudness


def distinct(key, rows, number_of, top, lift):
    sequence = jax.random.permutation(jax.random.fold_in(key, 1), number_of)
    favour = sequence
    for power in range(3):
        favour = favour * favour // number_of
    favour = favour * lift // number_of
    chance = jax.random.randint(jax.random.fold_in(key, 2), (rows, number_of), 0, 4096) + favour
    sure = jax.random.permutation(jax.random.fold_in(key, 3), rows)[jnp.arange(number_of) % rows]
    chance = jnp.where(jnp.arange(rows)[:, None] == sure[None, :], 1 << 14, chance)
    score = chance * number_of + jnp.arange(number_of)
    return lax.top_k(score.astype(jnp.int32), top)[1].astype(jnp.int32)


def scatter_about(rng, extent, scale, limit, split=(), kind=jnp.bfloat16):
    drawn = jax.random.normal(rng, extent, jnp.float32) * scale
    if len(split) > 0:
        drawn = block_scale(rng, extent, split, -0.22, 0.18) * drawn
    return jnp.clip(drawn, min=-limit, max=limit).astype(kind)


def setup_inputs(seed: int = 0) -> dict:
    arg_keys = jax.random.split(jax.random.key(seed), 7)
    return {
        "tokens": scatter_about(arg_keys[0], (N_DP, TOKENS, D), 1.0, 6.0, ((0, 16), (1, 16))),
        "cotangent": scatter_about(arg_keys[1], (N_DP, TOKENS, FF), 1.0, 6.0, ((0, 16), (1, 16))),
        "weights": scatter_about(arg_keys[2], (N_DP, FFB, 2, KB, BLOCK, BLOCK), 1.0, 6.0, ((0, 16), (1, 16))),
        "momentum": scatter_about(arg_keys[3], (N_DP, FFB, 2, KB, BLOCK, BLOCK), 0.5, 4.0, ((0, 16), (1, 16))),
        "pattern": distinct(arg_keys[4], FFB, DB, KB, 0),
        "step": jax.random.randint(arg_keys[5], (), 0, 4096).astype(jnp.int32),
    }


def replica_step(pattern_flat, operands):
    tok_rows, cot_rows, packed, moment = operands
    scale = (KB * BLOCK) ** -0.5
    chosen = jnp.take(tok_rows.reshape(TOKENS, DB, BLOCK), pattern_flat, axis=1)
    chosen = chosen.reshape(TOKENS, FFB, KB, BLOCK).astype(jnp.float32)
    weights_f = packed.astype(jnp.float32)
    gate = jnp.einsum("rjkc,jkcf->rjf", chosen, weights_f[:, 0]) * scale
    up_val = jnp.einsum("rjkc,jkcf->rjf", chosen, weights_f[:, 1]) * scale
    sigma = jax.nn.sigmoid(gate)
    hidden = (gate * sigma * up_val).astype(jnp.bfloat16).reshape(TOKENS, FF)
    back = cot_rows.reshape(TOKENS, FFB, BLOCK).astype(jnp.float32)
    dgate = (back * up_val * sigma * (1.0 + gate * (1.0 - sigma))).astype(jnp.bfloat16)
    duptail = (back * gate * sigma).astype(jnp.bfloat16)
    grad_gate = jnp.einsum("rjkc,rjf->jkcf", chosen, dgate.astype(jnp.float32)) * scale
    grad_up = jnp.einsum("rjkc,rjf->jkcf", chosen, duptail.astype(jnp.float32)) * scale
    grad = jnp.stack([grad_gate, grad_up], axis=1)
    moved = (0.9 * moment.astype(jnp.float32) + grad).astype(jnp.bfloat16)
    stepped = (packed.astype(jnp.float32) - 0.1 * moved.astype(jnp.float32)).astype(jnp.bfloat16)
    return hidden, stepped, moved


def reference(tokens, cotangent, weights, momentum, pattern, step):
    pattern_flat = pattern.reshape(-1).astype(jnp.int32)
    hidden, stepped, moved = lax.map(partial(replica_step, pattern_flat), (tokens, cotangent, weights, momentum))
    levels = N_DP.bit_length() - 1
    distance = jnp.left_shift(jnp.int32(1), (step % levels).astype(jnp.int32))
    far_weights = jnp.roll(stepped, distance, axis=0)
    far_moment = jnp.roll(moved, distance, axis=0)
    new_weights = ((stepped.astype(jnp.float32) + far_weights.astype(jnp.float32)) * 0.5).astype(jnp.bfloat16)
    new_momentum = ((moved.astype(jnp.float32) + far_moment.astype(jnp.float32)) * 0.5).astype(jnp.bfloat16)
    return hidden, new_weights, new_momentum
```

```python
from functools import partial

import jax
import jax.numpy as jnp
from jax import lax
from jax.experimental import pallas as pl
from jax.experimental.pallas import tpu as pltpu
from jax.sharding import PartitionSpec as P

BLOCK = 128
KB = 2
SCALE = (KB * BLOCK) ** -0.5
MIB = 1 << 20
VMEM = pl.BlockSpec(memory_space=pltpu.VMEM)


def split_kernel(width, cot_ref, out_ref):
    for t in range(out_ref.shape[0]):
        out_ref[t] = cot_ref[:, t * width : (t + 1) * width]


def split_columns(cot, groups):
    rows, columns = cot.shape
    width = columns // groups
    per = 4
    return pl.pallas_call(
        partial(split_kernel, width),
        grid=(groups // per,),
        out_shape=jax.ShapeDtypeStruct((groups, rows, width), cot.dtype),
        in_specs=[pl.BlockSpec((rows, per * width), lambda g: (0, g))],
        out_specs=pl.BlockSpec((per, rows, width), lambda g: (g, 0, 0)),
        cost_estimate=pl.CostEstimate(flops=0, bytes_accessed=4 * cot.size, transcendentals=0),
    )(cot)


def join_kernel(width, in_ref, out_ref):
    for t in range(in_ref.shape[0]):
        out_ref[:, t * width : (t + 1) * width] = in_ref[t]


def join_columns(parts):
    groups, rows, width = parts.shape
    per = 4
    return pl.pallas_call(
        partial(join_kernel, width),
        grid=(groups // per,),
        out_shape=jax.ShapeDtypeStruct((rows, groups * width), parts.dtype),
        in_specs=[pl.BlockSpec((per, rows, width), lambda g: (g, 0, 0))],
        out_specs=pl.BlockSpec((rows, per * width), lambda g: (0, g)),
        cost_estimate=pl.CostEstimate(flops=0, bytes_accessed=4 * parts.size, transcendentals=0),
    )(parts)


def pick_kernel(slots, pattern_ref, tok_ref, out_ref):
    per = out_ref.shape[0]
    first = pl.program_id(0) * per * slots
    for t in range(per):
        for s in range(slots):
            at = pl.multiple_of(pattern_ref[first + t * slots + s] * BLOCK, BLOCK)
            out_ref[t, :, s * BLOCK : (s + 1) * BLOCK] = tok_ref[:, pl.ds(at, BLOCK)]


def pick_blocks(pattern_flat, tok, groups):
    rows, columns = tok.shape
    slots = pattern_flat.shape[0] // groups
    per = 4
    out = jax.ShapeDtypeStruct((groups, rows, slots * BLOCK), tok.dtype)
    return pl.pallas_call(
        partial(pick_kernel, slots),
        grid_spec=pltpu.PrefetchScalarGridSpec(
            num_scalar_prefetch=1,
            grid=(groups // per,),
            in_specs=[pl.BlockSpec((rows, columns), lambda g, pattern: (0, 0))],
            out_specs=pl.BlockSpec((per, rows, slots * BLOCK), lambda g, pattern: (g, 0, 0)),
        ),
        out_shape=out,
        cost_estimate=pl.CostEstimate(flops=0, bytes_accessed=4 * out.size, transcendentals=0),
    )(pattern_flat, tok)


def block_kernel(sel_ref, cot_ref, weight_ref, moment_ref, _, hidden_ref, moved_ref, slope_ref):
    rows = sel_ref.shape[0]
    step = 256
    packed = jnp.concatenate([weight_ref[0, 0], weight_ref[0, 1]], axis=1)
    for r in range(0, rows, step):
        at = slice(r, r + step)
        both = jnp.dot(sel_ref[at, :], packed, preferred_element_type=jnp.float32) * SCALE
        gate, up = both[:, :BLOCK], both[:, BLOCK:]
        sigma = jax.nn.sigmoid(gate)
        swish = gate * sigma
        hidden_ref[at, :] = (swish * up).astype(hidden_ref.dtype)
        back = cot_ref[at, :].astype(jnp.float32)
        slope_ref[at, :BLOCK] = (back * up * sigma * (1.0 + gate * (1.0 - sigma))).astype(jnp.bfloat16)
        slope_ref[at, BLOCK:] = (back * swish).astype(jnp.bfloat16)
    grad = (
        lax.dot_general(
            sel_ref[...], slope_ref[...], (((0,), (0,)), ((), ())), preferred_element_type=jnp.float32
        )
        * SCALE
    )
    for kind in range(2):
        part = grad[:, kind * BLOCK : (kind + 1) * BLOCK]
        moved = 0.9 * moment_ref[0, kind].astype(jnp.float32) + part
        moved_ref[0, kind] = moved.astype(moved_ref.dtype)


def block_step(sel, cot, weights, moment, after):
    rows, width = cot.shape
    blocks = width // BLOCK
    depth = KB * BLOCK
    by_column = lambda j: (0, j)
    by_block = lambda j: (j, 0, 0, 0)
    return pl.pallas_call(
        block_kernel,
        grid=(blocks,),
        out_shape=(
            jax.ShapeDtypeStruct((rows, width), jnp.bfloat16),
            jax.ShapeDtypeStruct(moment.shape, jnp.bfloat16),
        ),
        in_specs=[
            pl.BlockSpec((rows, depth), by_column),
            pl.BlockSpec((rows, BLOCK), by_column),
            pl.BlockSpec((1, 2, depth, BLOCK), by_block),
            pl.BlockSpec((1, 2, depth, BLOCK), by_block),
            pl.BlockSpec(memory_space=pl.ANY),
        ],
        out_specs=(
            pl.BlockSpec((rows, BLOCK), by_column),
            pl.BlockSpec((1, 2, depth, BLOCK), by_block),
        ),
        scratch_shapes=[pltpu.VMEM((rows, 2 * BLOCK), jnp.bfloat16)],
        compiler_params=pltpu.CompilerParams(vmem_limit_bytes=32 * MIB),
        cost_estimate=pl.CostEstimate(
            flops=8 * rows * depth * width,
            bytes_accessed=2 * (sel.size + 2 * cot.size + 3 * moment.size),
            transcendentals=2 * cot.size,
        ),
    )(sel, cot, weights, moment, after)


def exchange(value):
    return lax.all_to_all(value, "tensor", split_axis=0, concat_axis=0, tiled=True)


def with_distance(distance, tok, cot, weights, moment, pattern):
    replicas = lax.axis_size("dp")
    groups = lax.axis_size("tensor")
    pairs = [(i, (i + distance) % replicas) for i in range(replicas)]
    rows = tok.shape[0] * groups
    far_weights = lax.ppermute(weights, "dp", pairs)
    cot_rows = exchange(split_columns(cot, groups)).reshape(rows, -1)
    pattern_flat = lax.all_gather(pattern, "tensor", axis=0, tiled=True).reshape(-1)
    sel_rows = exchange(pick_blocks(pattern_flat, tok, groups)).reshape(rows, -1)
    hidden, moved = block_step(sel_rows, cot_rows, weights, moment, far_weights)
    far_moved = lax.ppermute(moved, "dp", pairs)
    hidden = join_columns(exchange(hidden.reshape(groups, tok.shape[0], -1)))

    def stepped(w, m):
        w = w.astype(jnp.float32) - 0.1 * m.astype(jnp.float32)
        return w.astype(jnp.bfloat16).astype(jnp.float32)

    new_weights = (stepped(weights, moved) + stepped(far_weights, far_moved)) * 0.5
    new_moment = (moved.astype(jnp.float32) + far_moved.astype(jnp.float32)) * 0.5
    return hidden, new_weights.astype(jnp.bfloat16), new_moment.astype(jnp.bfloat16)


def per_device(tokens, cotangent, weights, momentum, pattern, step):
    shape = weights.shape
    packed = (shape[1], 2, KB * BLOCK, BLOCK)
    levels = lax.axis_size("dp").bit_length() - 1
    branches = [partial(with_distance, 2**level) for level in range(levels)]
    hidden, new_weights, new_moment = lax.switch(
        step % levels,
        branches,
        tokens[0],
        cotangent[0],
        weights.reshape(packed),
        momentum.reshape(packed),
        pattern,
    )
    return hidden[None], new_weights.reshape(shape), new_moment.reshape(shape)


def solution(mesh):
    blocks = P("dp", "tensor", None, None, None, None)
    rows = P("dp", "tensor", None)
    return jax.shard_map(
        per_device,
        mesh=mesh,
        in_specs=(rows, rows, blocks, blocks, P("tensor", None), P()),
        out_specs=(rows, blocks, blocks),
        check_vma=False,
    )
```

```python
from functools import partial

import jax
import jax.numpy as jnp
from jax import lax
from jax.experimental import pallas as pl
from jax.experimental.pallas import tpu as pltpu
from jax.sharding import PartitionSpec as P

BLOCK = 128
KB = 2
SCALE = (KB * BLOCK) ** -0.5
MIB = 1 << 20
NAME_ROWS = 16
MIX_FLOPS = 40_000_000_000
ROWS_AT_ONCE = 256
ANY = pl.BlockSpec(memory_space=pl.ANY)


def through(groups, source, held, target, in_sems, out_sems):
    first = [pltpu.make_async_copy(source(t), held.at[t], in_sems.at[t]) for t in range(groups)]
    second = [pltpu.make_async_copy(held.at[t], target(t), out_sems.at[t]) for t in range(groups)]
    for copy in first:
        copy.start()
    for t in range(groups):
        first[t].wait()
        second[t].start()
    for copy in second:
        copy.wait()


def lay_kernel(pattern_ref, cot_ref, out_ref, came, held, in_sems, out_sems):
    groups, rows, width = came.shape
    blocks = width // BLOCK
    first = [
        pltpu.make_async_copy(cot_ref.at[:, pl.ds(t * width, width)], came.at[t], in_sems.at[t]) for t in range(groups)
    ]
    second = [pltpu.make_async_copy(held.at[t], out_ref.at[t], out_sems.at[t]) for t in range(groups)]
    for copy in first:
        copy.start()
    lane = lax.broadcasted_iota(jnp.int32, (NAME_ROWS, BLOCK), 1)
    named = jnp.zeros((NAME_ROWS, BLOCK), jnp.int32)
    for j in range(blocks):
        for i in range(KB):
            named = jnp.where(lane == j * KB + i, pattern_ref[i, j], named)
    named = named.astype(jnp.float32).astype(held.dtype)
    for t in range(groups):
        held[t, blocks * rows :, :] = named
        first[t].wait()
        for j in range(blocks):
            held[t, j * rows : (j + 1) * rows, :] = came[t, :, j * BLOCK : (j + 1) * BLOCK]
        second[t].start()
    for copy in second:
        copy.wait()


def lay_cotangent(pattern, cot, groups):
    rows, columns = cot.shape
    width = columns // groups
    shape = (groups, width // BLOCK * rows + NAME_ROWS, BLOCK)
    return pl.pallas_call(
        lay_kernel,
        out_shape=jax.ShapeDtypeStruct(shape, cot.dtype),
        in_specs=[pl.BlockSpec(memory_space=pltpu.SMEM), ANY],
        out_specs=ANY,
        scratch_shapes=[
            pltpu.VMEM((groups, rows, width), cot.dtype),
            pltpu.VMEM(shape, cot.dtype),
            pltpu.SemaphoreType.DMA((groups,)),
            pltpu.SemaphoreType.DMA((groups,)),
        ],
        cost_estimate=pl.CostEstimate(flops=0, bytes_accessed=4 * cot.size, transcendentals=0),
    )(pattern.T, cot)


def join_kernel(in_ref, out_ref, held, in_sems, out_sems):
    groups, _, width = held.shape
    through(
        groups,
        lambda t: in_ref.at[t],
        held,
        lambda t: out_ref.at[:, pl.ds(t * width, width)],
        in_sems,
        out_sems,
    )


def join_columns(parts):
    groups, rows, width = parts.shape
    return pl.pallas_call(
        join_kernel,
        out_shape=jax.ShapeDtypeStruct((rows, groups * width), parts.dtype),
        in_specs=[ANY],
        out_specs=ANY,
        scratch_shapes=[
            pltpu.VMEM(parts.shape, parts.dtype),
            pltpu.SemaphoreType.DMA((groups,)),
            pltpu.SemaphoreType.DMA((groups,)),
        ],
        cost_estimate=pl.CostEstimate(flops=0, bytes_accessed=4 * parts.size, transcendentals=0),
    )(parts)


def pick_kernel(pattern_ref, tok_ref, out_ref, held, sems):
    groups, _, width = held.shape
    slots = width // BLOCK
    copies = [pltpu.make_async_copy(held.at[t], out_ref.at[t], sems.at[t]) for t in range(groups)]
    for t in range(groups):
        for s in range(slots):
            at = pl.multiple_of(pattern_ref[t, s] * BLOCK, BLOCK)
            held[t, :, s * BLOCK : (s + 1) * BLOCK] = tok_ref[:, pl.ds(at, BLOCK)]
        copies[t].start()
    for copy in copies:
        copy.wait()


def pick_blocks(pattern, tok):
    groups, slots = pattern.shape
    out = jax.ShapeDtypeStruct((groups, tok.shape[0], slots * BLOCK), tok.dtype)
    return pl.pallas_call(
        pick_kernel,
        out_shape=out,
        in_specs=[pl.BlockSpec(memory_space=pltpu.SMEM), pl.BlockSpec(memory_space=pltpu.VMEM)],
        out_specs=ANY,
        scratch_shapes=[pltpu.VMEM(out.shape, tok.dtype), pltpu.SemaphoreType.DMA((groups,))],
        cost_estimate=pl.CostEstimate(flops=0, bytes_accessed=2 * tok.size + 2 * out.size, transcendentals=0),
    )(pattern, tok)


def block_kernel(sel_ref, cot_ref, weight_ref, moment_ref, _, hidden_ref, moved_ref, slope_ref, held, sems):
    blocks = weight_ref.shape[0]
    depth = KB * BLOCK
    groups = cot_ref.shape[0]
    each = sel_ref.shape[0] // groups
    step = ROWS_AT_ONCE
    copies = []
    for j in range(blocks):
        packed = jnp.concatenate([weight_ref[j, 0], weight_ref[j, 1]], axis=1) * jnp.bfloat16(SCALE)
        columns = slice(j * depth, (j + 1) * depth)
        for r in range(0, groups * each, step):
            at = slice(r, r + step)
            both = jnp.dot(sel_ref[at, columns], packed, preferred_element_type=jnp.float32)
            gate, up = both[:, :BLOCK], both[:, BLOCK:]
            sigma = jax.nn.sigmoid(gate)
            swish = gate * sigma
            held[j, at, :] = (swish * up).astype(held.dtype)
            back = cot_ref[r // each : (r + step) // each, j * each : (j + 1) * each, :]
            back = back.reshape(step, BLOCK).astype(jnp.float32)
            slope_ref[j % 2, at, :BLOCK] = (back * up * (sigma + swish * (1.0 - sigma))).astype(jnp.bfloat16)
            slope_ref[j % 2, at, BLOCK:] = (back * swish).astype(jnp.bfloat16)
        copies.append(
            pltpu.make_async_copy(held.at[j], hidden_ref.at[:, pl.ds(j * BLOCK, BLOCK)], sems.at[j])
        )
        copies[-1].start()
        grad = (
            lax.dot_general(
                sel_ref[:, columns],
                slope_ref[j % 2],
                (((0,), (0,)), ((), ())),
                preferred_element_type=jnp.float32,
            )
            * SCALE
        )
        for kind in range(2):
            part = grad[:, kind * BLOCK : (kind + 1) * BLOCK]
            moved = 0.9 * moment_ref[j, kind].astype(jnp.float32) + part
            moved_ref[j, kind] = moved.astype(moved_ref.dtype)
    for copy in copies:
        copy.wait()


def block_step(sel, cot, weights, moment, after):
    rows = sel.shape[0]
    blocks, _, depth, _ = weights.shape
    width = blocks * BLOCK
    whole = pl.BlockSpec(memory_space=pltpu.VMEM)
    return pl.pallas_call(
        block_kernel,
        out_shape=[
            jax.ShapeDtypeStruct((rows, width), jnp.bfloat16),
            jax.ShapeDtypeStruct(moment.shape, jnp.bfloat16),
        ],
        in_specs=[whole] * 4 + [ANY],
        out_specs=[ANY, whole],
        scratch_shapes=[
            pltpu.VMEM((2, rows, 2 * BLOCK), jnp.bfloat16),
            pltpu.VMEM((blocks, rows, BLOCK), jnp.bfloat16),
            pltpu.SemaphoreType.DMA((blocks,)),
        ],
        compiler_params=pltpu.CompilerParams(vmem_limit_bytes=60 * MIB),
        cost_estimate=pl.CostEstimate(
            flops=8 * rows * depth * width,
            bytes_accessed=2 * (sel.size + 2 * cot.size + 3 * moment.size),
            transcendentals=2 * rows * width,
        ),
    )(sel, cot, weights, moment, after)


def mix_kernel(moved_ref, far_moved_ref, weight_ref, far_weight_ref, new_weight_ref, new_moment_ref, held, sems):
    outs = (new_weight_ref, new_moment_ref)
    copies = []
    for j in range(moved_ref.shape[0]):
        moved, far_moved = moved_ref[j].astype(jnp.float32), far_moved_ref[j].astype(jnp.float32)
        both = []
        for ref, m in ((weight_ref, moved), (far_weight_ref, far_moved)):
            both.append((ref[j].astype(jnp.float32) - 0.1 * m).astype(jnp.bfloat16).astype(jnp.float32))
        held[0, j] = ((both[0] + both[1]) * 0.5).astype(held.dtype)
        held[1, j] = ((moved + far_moved) * 0.5).astype(held.dtype)
        for i, ref in enumerate(outs):
            copies.append(pltpu.make_async_copy(held.at[i, j], ref.at[j], sems.at[i, j]))
            copies[-1].start()
    for copy in copies:
        copy.wait()


def mix(moved, far_moved, weights, far_weights):
    whole = pl.BlockSpec(memory_space=pltpu.VMEM)
    return pl.pallas_call(
        mix_kernel,
        out_shape=[jax.ShapeDtypeStruct(weights.shape, weights.dtype)] * 2,
        in_specs=[whole] * 4,
        out_specs=[ANY] * 2,
        scratch_shapes=[
            pltpu.VMEM((2,) + weights.shape, weights.dtype),
            pltpu.SemaphoreType.DMA((2, weights.shape[0])),
        ],
        compiler_params=pltpu.CompilerParams(vmem_limit_bytes=16 * MIB),
        cost_estimate=pl.CostEstimate(flops=MIX_FLOPS, bytes_accessed=12 * moved.size, transcendentals=0),
    )(moved, far_moved, weights, far_weights)


def exchange(value):
    return lax.all_to_all(value, "tensor", split_axis=0, concat_axis=0, tiled=True)


def with_distance(distance, tok, cot, weights, moment, pattern):
    replicas = lax.axis_size("dp")
    groups = lax.axis_size("tensor")
    pairs = [(i, (i + distance) % replicas) for i in range(replicas)]
    rows = tok.shape[0] * groups
    far_weights = lax.ppermute(weights, "dp", pairs)
    cot_rows = exchange(lay_cotangent(pattern, cot, groups))
    patterns = cot_rows[:, -NAME_ROWS, : pattern.size].astype(jnp.int32)
    sel_rows = exchange(pick_blocks(patterns, tok)).reshape(rows, -1)
    hidden, moved = block_step(sel_rows, cot_rows, weights, moment, far_weights)
    far_moved = lax.ppermute(moved, "dp", pairs)
    hidden = join_columns(exchange(hidden.reshape(groups, tok.shape[0], -1)))

    return hidden, *mix(moved, far_moved, weights, far_weights)


def per_device(tokens, cotangent, weights, momentum, pattern, step):
    shape = weights.shape
    packed = (shape[1], 2, KB * BLOCK, BLOCK)
    levels = lax.axis_size("dp").bit_length() - 1
    branches = [partial(with_distance, 2**level) for level in range(levels)]
    hidden, new_weights, new_moment = lax.switch(
        step % levels,
        branches,
        tokens[0],
        cotangent[0],
        weights.reshape(packed),
        momentum.reshape(packed),
        pattern,
    )
    return hidden[None], new_weights.reshape(shape), new_moment.reshape(shape)


def solution(mesh):
    blocks = P("dp", "tensor", None, None, None, None)
    rows = P("dp", "tensor", None)
    return jax.shard_map(
        per_device,
        mesh=mesh,
        in_specs=(rows, rows, blocks, blocks, P("tensor", None), P()),
        out_specs=(rows, blocks, blocks),
        check_vma=False,
    )
```

```python
from functools import partial

import jax
import jax.numpy as jnp
from jax import lax
from jax.experimental import pallas as pl
from jax.experimental.pallas import tpu as pltpu
from jax.sharding import PartitionSpec as P

BLOCK = 128
KB = 2
SCALE = (KB * BLOCK) ** -0.5
MIB = 1 << 20
NAME_ROWS = 16
EARLY = (1, 2)
MIX_FLOPS = 40_000_000_000
ROWS_AT_ONCE = 256
ANY = pl.BlockSpec(memory_space=pl.ANY)


def through(groups, source, held, target, in_sems, out_sems):
    first = [pltpu.make_async_copy(source(t), held.at[t], in_sems.at[t]) for t in range(groups)]
    second = [pltpu.make_async_copy(held.at[t], target(t), out_sems.at[t]) for t in range(groups)]
    for copy in first:
        copy.start()
    for t in range(groups):
        first[t].wait()
        second[t].start()
    for copy in second:
        copy.wait()


def lay_kernel(pattern_ref, cot_ref, out_ref, came, held, in_sems, out_sems):
    groups, rows, width = came.shape
    blocks = width // BLOCK
    first = [
        pltpu.make_async_copy(cot_ref.at[:, pl.ds(t * width, width)], came.at[t], in_sems.at[t]) for t in range(groups)
    ]
    second = [pltpu.make_async_copy(held.at[t], out_ref.at[t], out_sems.at[t]) for t in range(groups)]
    for copy in first:
        copy.start()
    lane = lax.broadcasted_iota(jnp.int32, (NAME_ROWS, BLOCK), 1)
    named = jnp.zeros((NAME_ROWS, BLOCK), jnp.int32)
    for j in range(blocks):
        for i in range(KB):
            named = jnp.where(lane == j * KB + i, pattern_ref[i, j], named)
    named = named.astype(jnp.float32).astype(held.dtype)

    def one_device(t, carry):
        held[t, blocks * rows :, :] = named
        pltpu.make_async_copy(
            cot_ref.at[:, pl.ds(pl.multiple_of(t * width, BLOCK), width)], came.at[t], in_sems.at[t]
        ).wait()
        for j in range(blocks):
            held[t, j * rows : (j + 1) * rows, :] = came[t, :, j * BLOCK : (j + 1) * BLOCK]
        pltpu.make_async_copy(held.at[t], out_ref.at[t], out_sems.at[t]).start()
        return carry

    lax.fori_loop(0, groups, one_device, 0)
    for copy in second:
        copy.wait()


def lay_cotangent(pattern, cot, groups):
    rows, columns = cot.shape
    width = columns // groups
    shape = (groups, width // BLOCK * rows + NAME_ROWS, BLOCK)
    return pl.pallas_call(
        lay_kernel,
        out_shape=jax.ShapeDtypeStruct(shape, cot.dtype),
        in_specs=[pl.BlockSpec(memory_space=pltpu.SMEM), ANY],
        out_specs=ANY,
        scratch_shapes=[
            pltpu.VMEM((groups, rows, width), cot.dtype),
            pltpu.VMEM(shape, cot.dtype),
            pltpu.SemaphoreType.DMA((groups,)),
            pltpu.SemaphoreType.DMA((groups,)),
        ],
        cost_estimate=pl.CostEstimate(flops=0, bytes_accessed=4 * cot.size, transcendentals=0),
    )(pattern.T, cot)


def join_kernel(in_ref, out_ref, held, in_sems, out_sems):
    groups, _, width = held.shape
    through(
        groups,
        lambda t: in_ref.at[t],
        held,
        lambda t: out_ref.at[:, pl.ds(t * width, width)],
        in_sems,
        out_sems,
    )


def join_columns(parts):
    groups, rows, width = parts.shape
    return pl.pallas_call(
        join_kernel,
        out_shape=pltpu.HBM((rows, groups * width), parts.dtype),
        in_specs=[ANY],
        out_specs=ANY,
        scratch_shapes=[
            pltpu.VMEM(parts.shape, parts.dtype),
            pltpu.SemaphoreType.DMA((groups,)),
            pltpu.SemaphoreType.DMA((groups,)),
        ],
        cost_estimate=pl.CostEstimate(flops=0, bytes_accessed=4 * parts.size, transcendentals=0),
    )(parts)


def pick_kernel(pattern_ref, tok_ref, *refs):
    out_ref, held, sems = refs[-3:]
    groups, _, width = held.shape
    slots = width // BLOCK
    copies = [pltpu.make_async_copy(held.at[t], out_ref.at[t], sems.at[t]) for t in range(groups)]

    def one_device(t, carry):
        for s in range(slots):
            at = pl.multiple_of(pattern_ref[t, s] * BLOCK, BLOCK)
            held[t, :, s * BLOCK : (s + 1) * BLOCK] = tok_ref[:, pl.ds(at, BLOCK)]
        pltpu.make_async_copy(held.at[t], out_ref.at[t], sems.at[t]).start()
        return carry

    lax.fori_loop(0, groups, one_device, 0)
    for copy in copies:
        copy.wait()


def pick_blocks(pattern, tok, *after):
    groups, slots = pattern.shape
    out = jax.ShapeDtypeStruct((groups, tok.shape[0], slots * BLOCK), tok.dtype)
    return pl.pallas_call(
        pick_kernel,
        out_shape=out,
        in_specs=[pl.BlockSpec(memory_space=pltpu.SMEM), pl.BlockSpec(memory_space=pltpu.VMEM)] + [ANY] * len(after),
        out_specs=ANY,
        scratch_shapes=[pltpu.VMEM(out.shape, tok.dtype), pltpu.SemaphoreType.DMA((groups,))],
        cost_estimate=pl.CostEstimate(flops=0, bytes_accessed=2 * tok.size + 2 * out.size, transcendentals=0),
    )(pattern, tok, *after)


def block_kernel(sel_ref, cot_ref, weight_ref, moment_ref, _, hidden_ref, moved_ref, slope_ref, held, sems):
    blocks = weight_ref.shape[0]
    depth = KB * BLOCK
    groups = cot_ref.shape[0]
    each = sel_ref.shape[0] // groups
    step = ROWS_AT_ONCE
    copies = []
    for j in range(blocks):
        packed = jnp.concatenate([weight_ref[j, 0], weight_ref[j, 1]], axis=1) * jnp.bfloat16(SCALE)
        columns = slice(j * depth, (j + 1) * depth)
        for r in range(0, groups * each, step):
            at = slice(r, r + step)
            both = jnp.dot(sel_ref[at, columns], packed, preferred_element_type=jnp.float32)
            gate, up = both[:, :BLOCK], both[:, BLOCK:]
            sigma = jax.nn.sigmoid(gate)
            swish = gate * sigma
            held[j, at, :] = (swish * up).astype(held.dtype)
            back = cot_ref[r // each : (r + step) // each, j * each : (j + 1) * each, :]
            back = back.reshape(step, BLOCK).astype(jnp.float32)
            slope_ref[j % 2, at, :BLOCK] = (back * up * (sigma + swish * (1.0 - sigma))).astype(jnp.bfloat16)
            slope_ref[j % 2, at, BLOCK:] = (back * swish).astype(jnp.bfloat16)
        copies.append(
            pltpu.make_async_copy(held.at[j], hidden_ref.at[:, pl.ds(j * BLOCK, BLOCK)], sems.at[j])
        )
        copies[-1].start()
        grad = (
            lax.dot_general(
                sel_ref[:, columns],
                slope_ref[j % 2],
                (((0,), (0,)), ((), ())),
                preferred_element_type=jnp.float32,
            )
            * SCALE
        )
        for kind in range(2):
            part = grad[:, kind * BLOCK : (kind + 1) * BLOCK]
            moved = 0.9 * moment_ref[j, kind].astype(jnp.float32) + part
            moved_ref[j, kind] = moved.astype(moved_ref.dtype)
    for copy in copies:
        copy.wait()


def block_step(sel, cot, weights, moment, after):
    rows = sel.shape[0]
    blocks, _, depth, _ = weights.shape
    width = blocks * BLOCK
    whole = pl.BlockSpec(memory_space=pltpu.VMEM)
    return pl.pallas_call(
        block_kernel,
        out_shape=[
            pltpu.HBM((rows, width), jnp.bfloat16),
            jax.ShapeDtypeStruct(moment.shape, jnp.bfloat16),
        ],
        in_specs=[whole] * 4 + [ANY],
        out_specs=[ANY, whole],
        scratch_shapes=[
            pltpu.VMEM((2, rows, 2 * BLOCK), jnp.bfloat16),
            pltpu.VMEM((blocks, rows, BLOCK), jnp.bfloat16),
            pltpu.SemaphoreType.DMA((blocks,)),
        ],
        compiler_params=pltpu.CompilerParams(vmem_limit_bytes=32 * MIB),
        cost_estimate=pl.CostEstimate(
            flops=8 * rows * depth * width,
            bytes_accessed=2 * (sel.size + 2 * cot.size + 3 * moment.size),
            transcendentals=2 * rows * width,
        ),
    )(sel, cot, weights, moment, after)


def mix_kernel(moved_ref, far_moved_ref, weight_ref, far_weight_ref, new_weight_ref, new_moment_ref, held, sems):
    outs = (new_weight_ref, new_moment_ref)
    blocks = moved_ref.shape[0]

    def leaving(j):
        return [pltpu.make_async_copy(held.at[i, j], ref.at[j], sems.at[i, j]) for i, ref in enumerate(outs)]

    def one_block(j, carry):
        moved, far_moved = moved_ref[j].astype(jnp.float32), far_moved_ref[j].astype(jnp.float32)
        both = []
        for ref, m in ((weight_ref, moved), (far_weight_ref, far_moved)):
            both.append((ref[j].astype(jnp.float32) - 0.1 * m).astype(jnp.bfloat16).astype(jnp.float32))
        held[0, j] = ((both[0] + both[1]) * 0.5).astype(held.dtype)
        held[1, j] = ((moved + far_moved) * 0.5).astype(held.dtype)
        for copy in leaving(j):
            copy.start()
        return carry

    lax.fori_loop(0, blocks, one_block, 0)
    for j in range(blocks):
        for copy in leaving(j):
            copy.wait()


def mix(moved, far_moved, weights, far_weights):
    whole = pl.BlockSpec(memory_space=pltpu.VMEM)
    return pl.pallas_call(
        mix_kernel,
        out_shape=[jax.ShapeDtypeStruct(weights.shape, weights.dtype)] * 2,
        in_specs=[whole] * 4,
        out_specs=[ANY] * 2,
        scratch_shapes=[
            pltpu.VMEM((2,) + weights.shape, weights.dtype),
            pltpu.SemaphoreType.DMA((2, weights.shape[0])),
        ],
        compiler_params=pltpu.CompilerParams(vmem_limit_bytes=16 * MIB),
        cost_estimate=pl.CostEstimate(flops=MIX_FLOPS, bytes_accessed=12 * moved.size, transcendentals=0),
    )(moved, far_moved, weights, far_weights)


def exchange(value):
    return lax.all_to_all(value, "tensor", split_axis=0, concat_axis=0, tiled=True)


def with_distance(distance, tok, cot, weights, moment, pattern):
    replicas = lax.axis_size("dp")
    groups = lax.axis_size("tensor")
    pairs = [(i, (i + distance) % replicas) for i in range(replicas)]
    rows = tok.shape[0] * groups
    far_weights = lax.ppermute(weights, "dp", pairs)
    cot_rows = exchange(lay_cotangent(pattern, cot, groups))
    patterns = cot_rows[:, -NAME_ROWS, : pattern.size].astype(jnp.int32)
    early = [far_weights] if distance in EARLY else []
    sel_rows = exchange(pick_blocks(patterns, tok, *early)).reshape(rows, -1)
    hidden, moved = block_step(sel_rows, cot_rows, weights, moment, far_weights)
    far_moved = lax.ppermute(moved, "dp", pairs)
    hidden = join_columns(exchange(hidden.reshape(groups, tok.shape[0], -1)))

    return hidden, *mix(moved, far_moved, weights, far_weights)


def per_device(tokens, cotangent, weights, momentum, pattern, step):
    shape = weights.shape
    packed = (shape[1], 2, KB * BLOCK, BLOCK)
    levels = lax.axis_size("dp").bit_length() - 1
    branches = [partial(with_distance, 2**level) for level in range(levels)]
    hidden, new_weights, new_moment = lax.switch(
        step % levels,
        branches,
        tokens[0],
        cotangent[0],
        weights.reshape(packed),
        momentum.reshape(packed),
        pattern,
    )
    return hidden[None], new_weights.reshape(shape), new_moment.reshape(shape)


def solution(mesh):
    blocks = P("dp", "tensor", None, None, None, None)
    rows = P("dp", "tensor", None)
    return jax.shard_map(
        per_device,
        mesh=mesh,
        in_specs=(rows, rows, blocks, blocks, P("tensor", None), P()),
        out_specs=(rows, blocks, blocks),
        check_vma=False,
    )
```

```python
from functools import partial

import jax
import jax.numpy as jnp
from jax import lax
from jax.experimental import pallas as pl
from jax.experimental.pallas import tpu as pltpu
from jax.sharding import PartitionSpec as P

BLOCK = 128
KB = 2
SCALE = (KB * BLOCK) ** -0.5
MIB = 1 << 20
NAME_ROWS = 16
EARLY = (1, 2)
MIX_FLOPS = 40_000_000_000
ROWS_AT_ONCE = 256
ANY = pl.BlockSpec(memory_space=pl.ANY)


def through(groups, source, held, target, in_sems, out_sems):
    first = [pltpu.make_async_copy(source(t), held.at[t], in_sems.at[t]) for t in range(groups)]
    second = [pltpu.make_async_copy(held.at[t], target(t), out_sems.at[t]) for t in range(groups)]
    for copy in first:
        copy.start()
    for t in range(groups):
        first[t].wait()
        second[t].start()
    for copy in second:
        copy.wait()


def lay_kernel(pattern_ref, cot_ref, out_ref, came, held, in_sems, out_sems):
    groups, rows, width = came.shape
    blocks = width // BLOCK
    first = [
        pltpu.make_async_copy(cot_ref.at[:, pl.ds(t * width, width)], came.at[t], in_sems.at[t]) for t in range(groups)
    ]
    second = [pltpu.make_async_copy(held.at[t], out_ref.at[t], out_sems.at[t]) for t in range(groups)]
    for copy in first:
        copy.start()
    lane = lax.broadcasted_iota(jnp.int32, (NAME_ROWS, BLOCK), 1)
    named = jnp.zeros((NAME_ROWS, BLOCK), jnp.int32)
    for j in range(blocks):
        for i in range(KB):
            named = jnp.where(lane == j * KB + i, pattern_ref[i, j], named)
    named = named.astype(jnp.float32).astype(held.dtype)

    def one_device(t, carry):
        held[t, blocks * rows :, :] = named
        pltpu.make_async_copy(
            cot_ref.at[:, pl.ds(pl.multiple_of(t * width, BLOCK), width)], came.at[t], in_sems.at[t]
        ).wait()
        for j in range(blocks):
            held[t, j * rows : (j + 1) * rows, :] = came[t, :, j * BLOCK : (j + 1) * BLOCK]
        pltpu.make_async_copy(held.at[t], out_ref.at[t], out_sems.at[t]).start()
        return carry

    lax.fori_loop(0, groups, one_device, 0)
    for copy in second:
        copy.wait()


def lay_cotangent(pattern, cot, groups):
    rows, columns = cot.shape
    width = columns // groups
    shape = (groups, width // BLOCK * rows + NAME_ROWS, BLOCK)
    return pl.pallas_call(
        lay_kernel,
        out_shape=jax.ShapeDtypeStruct(shape, cot.dtype),
        in_specs=[pl.BlockSpec(memory_space=pltpu.SMEM), ANY],
        out_specs=ANY,
        scratch_shapes=[
            pltpu.VMEM((groups, rows, width), cot.dtype),
            pltpu.VMEM(shape, cot.dtype),
            pltpu.SemaphoreType.DMA((groups,)),
            pltpu.SemaphoreType.DMA((groups,)),
        ],
        cost_estimate=pl.CostEstimate(flops=0, bytes_accessed=4 * cot.size, transcendentals=0),
    )(pattern.T, cot)


def join_kernel(in_ref, out_ref, held, in_sems, out_sems):
    groups, _, width = held.shape
    through(
        groups,
        lambda t: in_ref.at[t],
        held,
        lambda t: out_ref.at[:, pl.ds(t * width, width)],
        in_sems,
        out_sems,
    )


def join_columns(parts):
    groups, rows, width = parts.shape
    return pl.pallas_call(
        join_kernel,
        out_shape=pltpu.HBM((rows, groups * width), parts.dtype),
        in_specs=[ANY],
        out_specs=ANY,
        scratch_shapes=[
            pltpu.VMEM(parts.shape, parts.dtype),
            pltpu.SemaphoreType.DMA((groups,)),
            pltpu.SemaphoreType.DMA((groups,)),
        ],
        cost_estimate=pl.CostEstimate(flops=0, bytes_accessed=4 * parts.size, transcendentals=0),
    )(parts)


def pick_kernel(pattern_ref, tok_ref, *refs):
    out_ref, held, sems = refs[-3:]
    groups, _, width = held.shape
    slots = width // BLOCK
    copies = [pltpu.make_async_copy(held.at[t], out_ref.at[t], sems.at[t]) for t in range(groups)]

    def one_device(t, carry):
        for s in range(slots):
            at = pl.multiple_of(pattern_ref[t, s] * BLOCK, BLOCK)
            held[t, :, s * BLOCK : (s + 1) * BLOCK] = tok_ref[:, pl.ds(at, BLOCK)]
        pltpu.make_async_copy(held.at[t], out_ref.at[t], sems.at[t]).start()
        return carry

    lax.fori_loop(0, groups, one_device, 0)
    for copy in copies:
        copy.wait()


def pick_blocks(pattern, tok, *after):
    groups, slots = pattern.shape
    out = jax.ShapeDtypeStruct((groups, tok.shape[0], slots * BLOCK), tok.dtype)
    return pl.pallas_call(
        pick_kernel,
        out_shape=out,
        in_specs=[pl.BlockSpec(memory_space=pltpu.SMEM), pl.BlockSpec(memory_space=pltpu.VMEM)] + [ANY] * len(after),
        out_specs=ANY,
        scratch_shapes=[pltpu.VMEM(out.shape, tok.dtype), pltpu.SemaphoreType.DMA((groups,))],
        cost_estimate=pl.CostEstimate(flops=0, bytes_accessed=2 * tok.size + 2 * out.size, transcendentals=0),
    )(pattern, tok, *after)


def block_kernel(sel_ref, cot_ref, weight_ref, moment_ref, _, hidden_ref, moved_ref, slope_ref, held, sems):
    blocks = weight_ref.shape[0]
    depth = KB * BLOCK
    groups = cot_ref.shape[0]
    each = sel_ref.shape[0] // groups
    step = ROWS_AT_ONCE
    copies = []
    for j in range(blocks):
        packed = jnp.concatenate([weight_ref[j, 0], weight_ref[j, 1]], axis=1) * jnp.bfloat16(SCALE)
        columns = slice(j * depth, (j + 1) * depth)
        for r in range(0, groups * each, step):
            at = slice(r, r + step)
            both = jnp.dot(sel_ref[at, columns], packed, preferred_element_type=jnp.float32)
            gate, up = both[:, :BLOCK], both[:, BLOCK:]
            sigma = jax.nn.sigmoid(gate)
            swish = gate * sigma
            held[j, at, :] = (swish * up).astype(held.dtype)
            back = cot_ref[r // each : (r + step) // each, j * each : (j + 1) * each, :]
            back = back.reshape(step, BLOCK).astype(jnp.float32)
            slope_ref[j % 2, at, :BLOCK] = (back * up * (sigma + swish * (1.0 - sigma))).astype(jnp.bfloat16)
            slope_ref[j % 2, at, BLOCK:] = (back * swish).astype(jnp.bfloat16)
        copies.append(
            pltpu.make_async_copy(held.at[j], hidden_ref.at[:, pl.ds(j * BLOCK, BLOCK)], sems.at[j])
        )
        copies[-1].start()
        grad = (
            lax.dot_general(
                sel_ref[:, columns],
                slope_ref[j % 2],
                (((0,), (0,)), ((), ())),
                preferred_element_type=jnp.float32,
            )
            * SCALE
        )
        for kind in range(2):
            part = grad[:, kind * BLOCK : (kind + 1) * BLOCK]
            moved = 0.9 * moment_ref[j, kind].astype(jnp.float32) + part
            moved_ref[j, kind] = moved.astype(moved_ref.dtype)
    for copy in copies:
        copy.wait()


def block_step(sel, cot, weights, moment, after):
    rows = sel.shape[0]
    blocks, _, depth, _ = weights.shape
    width = blocks * BLOCK
    whole = pl.BlockSpec(memory_space=pltpu.VMEM)
    return pl.pallas_call(
        block_kernel,
        out_shape=[
            pltpu.HBM((rows, width), jnp.bfloat16),
            jax.ShapeDtypeStruct(moment.shape, jnp.bfloat16),
        ],
        in_specs=[whole] * 4 + [ANY],
        out_specs=[ANY, whole],
        scratch_shapes=[
            pltpu.VMEM((2, rows, 2 * BLOCK), jnp.bfloat16),
            pltpu.VMEM((blocks, rows, BLOCK), jnp.bfloat16),
            pltpu.SemaphoreType.DMA((blocks,)),
        ],
        compiler_params=pltpu.CompilerParams(vmem_limit_bytes=32 * MIB),
        cost_estimate=pl.CostEstimate(
            flops=8 * rows * depth * width,
            bytes_accessed=2 * (sel.size + 2 * cot.size + 3 * moment.size),
            transcendentals=2 * rows * width,
        ),
    )(sel, cot, weights, moment, after)


def mix_kernel(moved_ref, far_moved_ref, weight_ref, far_weight_ref, new_weight_ref, new_moment_ref, held, sems):
    outs = (new_weight_ref, new_moment_ref)
    blocks = moved_ref.shape[0]

    def leaving(j):
        return [pltpu.make_async_copy(held.at[i, j], ref.at[j], sems.at[i, j]) for i, ref in enumerate(outs)]

    def one_block(j, carry):
        moved, far_moved = moved_ref[j].astype(jnp.float32), far_moved_ref[j].astype(jnp.float32)
        both = []
        for ref, m in ((weight_ref, moved), (far_weight_ref, far_moved)):
            both.append((ref[j].astype(jnp.float32) - 0.1 * m).astype(jnp.bfloat16).astype(jnp.float32))
        held[0, j] = ((both[0] + both[1]) * 0.5).astype(held.dtype)
        held[1, j] = ((moved + far_moved) * 0.5).astype(held.dtype)
        for copy in leaving(j):
            copy.start()
        return carry

    lax.fori_loop(0, blocks, one_block, 0)
    for j in range(blocks):
        for copy in leaving(j):
            copy.wait()


def mix(moved, far_moved, weights, far_weights):
    whole = pl.BlockSpec(memory_space=pltpu.VMEM)
    return pl.pallas_call(
        mix_kernel,
        out_shape=[jax.ShapeDtypeStruct(weights.shape, weights.dtype)] * 2,
        in_specs=[whole] * 4,
        out_specs=[ANY] * 2,
        scratch_shapes=[
            pltpu.VMEM((2,) + weights.shape, weights.dtype),
            pltpu.SemaphoreType.DMA((2, weights.shape[0])),
        ],
        compiler_params=pltpu.CompilerParams(vmem_limit_bytes=16 * MIB),
        cost_estimate=pl.CostEstimate(flops=MIX_FLOPS, bytes_accessed=12 * moved.size, transcendentals=0),
    )(moved, far_moved, weights, far_weights)


def exchange(value):
    return lax.all_to_all(value, "tensor", split_axis=0, concat_axis=0, tiled=True)


def with_distance(distance, tok, cot, weights, moment, pattern):
    replicas = lax.axis_size("dp")
    groups = lax.axis_size("tensor")
    pairs = [(i, (i + distance) % replicas) for i in range(replicas)]
    rows = tok.shape[0] * groups
    far_weights = lax.ppermute(weights, "dp", pairs)
    cot_rows = exchange(lay_cotangent(pattern, cot, groups))
    patterns = cot_rows[:, -NAME_ROWS, : pattern.size].astype(jnp.int32)
    early = [far_weights[0, 0, :16]] if distance in EARLY else []
    sel_rows = exchange(pick_blocks(patterns, tok, *early)).reshape(rows, -1)
    hidden, moved = block_step(sel_rows, cot_rows, weights, moment, far_weights)
    far_moved = lax.ppermute(moved, "dp", pairs)
    hidden = join_columns(exchange(hidden.reshape(groups, tok.shape[0], -1)))

    return hidden, *mix(moved, far_moved, weights, far_weights)


def per_device(tokens, cotangent, weights, momentum, pattern, step):
    shape = weights.shape
    packed = (shape[1], 2, KB * BLOCK, BLOCK)
    levels = lax.axis_size("dp").bit_length() - 1
    branches = [partial(with_distance, 2**level) for level in range(levels)]
    hidden, new_weights, new_moment = lax.switch(
        step % levels,
        branches,
        tokens[0],
        cotangent[0],
        weights.reshape(packed),
        momentum.reshape(packed),
        pattern,
    )
    return hidden[None], new_weights.reshape(shape), new_moment.reshape(shape)


def solution(mesh):
    blocks = P("dp", "tensor", None, None, None, None)
    rows = P("dp", "tensor", None)
    return jax.shard_map(
        per_device,
        mesh=mesh,
        in_specs=(rows, rows, blocks, blocks, P("tensor", None), P()),
        out_specs=(rows, blocks, blocks),
        check_vma=False,
    )
```
